32 devices in a mesh: grp: 2 (over y), lon: 4 (over x, core), lat: 4 (over z).
Axes of the slice: x: 2, y: 2, z: 4, core: 2. Of those that a mesh axis runs over, the one named last changes fastest.
Arguments:
- grid_field: bfloat16 [192, 1440, 256], P(('grp', 'lat'), 'lon'), parts along dimension 0, may hold values from -6 to 6
- weights: bfloat16 [512, 2, 256, 256], P(('lon', 'lat')), may hold values from -0.25 to 0.25
Outputs:
- upsampled: bfloat16 [192, 2880, 256], P(('grp', 'lat'), 'lon'), parts along dimension 0
The draws below stay inside these ranges and needn't reach their ends.
There are 2 independent parts, one for each index of `grp`. The reference program is written for one: setup_inputs(seed, part) draws one part's arguments, and reference() takes and returns one part's arrays. A program takes and returns all parts, laid end to end along the dimension named above; an argument that names none is the same for every part. Nothing has to cross between parts.
All inputs are finite; a program needn't handle non-finite values.
Results may differ from the reference program's by a relative error of at most 0.014.
Values may be sent and summed in bfloat16 or wider, within the bound.
A program may use at most 320 MiB of HBM per device.

```python
import math
import jax
import jax.numpy as jnp
from jax import lax

NLON = 1440
C = 256
M = 512
NLAT = 96
NOUT = 2880
N_LON = 4


def level_of(stream_key, shape, split, low, high):
    factor_of = 1.0
    for position, shards_of in split:
        steps = jax.random.uniform(jax.random.fold_in(jax.random.fold_in(stream_key, 6), position), (shards_of,), jnp.float32, low / len(split), high / len(split))
        factor_of = factor_of * jnp.repeat(jnp.exp(steps), shape[position] // shards_of).reshape((-1,) + (1,) * (len(shape) - 1 - position))
    return factor_of


def centred(rng, extent, scale, most, split=(), kind=jnp.bfloat16):
    gain = level_of(rng, extent, split, -0.22, 0.18) if split else 1.0
    values = jax.random.normal(rng, extent, jnp.float32) * scale * gain
    return jnp.minimum(jnp.maximum(values, -most), most).astype(kind)


def setup_inputs(seed: int = 0, part: int = 0) -> dict:
    splits = jax.random.split(jax.random.key(seed), 3)
    own_keys = jax.random.split(jax.random.fold_in(splits[2], part), 3)
    grid_field = centred(own_keys[0], (NLAT, NLON, C), 1.0, 6.0, ((0, 4), (1, 4)))
    weights = centred(splits[1], (M, 2, C, C), (2 * C) ** -0.5, 0.25, ((0, 16),))
    return {"grid_field": grid_field, "weights": weights}


def tables():
    mode_index = jnp.arange(M, dtype=jnp.int32)
    lon_index = jnp.arange(NLON, dtype=jnp.int32)
    out_index = jnp.arange(NOUT, dtype=jnp.int32)
    norm_scale = 1.0 / math.sqrt(NLON)
    phase_index = mode_index[:, None] * lon_index[None, :] % NLON
    angles = 2.0 * math.pi / NLON * phase_index.astype(jnp.float32)
    analysis = jnp.stack([jnp.cos(angles) * norm_scale, -jnp.sin(angles) * norm_scale], 1)
    analysis = analysis.reshape(2 * M, NLON).astype(jnp.bfloat16)
    phase_out = mode_index[:, None] * out_index[None, :] % NOUT
    angles_out = 2.0 * math.pi / NOUT * phase_out.astype(jnp.float32)
    factor = jnp.where(mode_index == 0, 1.0, 2.0).astype(jnp.float32)[:, None] * norm_scale
    synthesis = jnp.stack([jnp.cos(angles_out) * factor, -jnp.sin(angles_out) * factor], 1)
    synthesis = synthesis.reshape(2 * M, NOUT).astype(jnp.bfloat16)
    return (analysis, synthesis)

def reference(grid_field, weights):
    analysis, synthesis = tables()
    lon_block = NLON // N_LON

    def add_block(running, block_idx):
        anchor = (block_idx * lon_block).astype(jnp.int32)
        grid_block = lax.dynamic_slice_in_dim(grid_field, anchor, lon_block, 1)
        table_block = lax.dynamic_slice_in_dim(analysis, anchor, lon_block, 1)
        flat_grid = grid_block.transpose(1, 0, 2).reshape(lon_block, NLAT * C)
        partial_value = jnp.dot(table_block, flat_grid, preferred_element_type=jnp.float32)
        partial_value = lax.optimization_barrier(partial_value.astype(jnp.bfloat16)).astype(jnp.float32)
        return (running + partial_value, None)
    start_sum = jnp.zeros((2 * M, NLAT * C), jnp.float32)
    running, _ = lax.scan(add_block, start_sum, jnp.arange(N_LON, dtype=jnp.int32))
    spectrum = running.astype(jnp.bfloat16).reshape(M, 2, NLAT, C)

    def mix_one(mode_item):
        spec_mode, weight_mode = mode_item
        real_in = spec_mode[0]
        imag_in = spec_mode[1]
        real_out = jnp.dot(real_in, weight_mode[0], preferred_element_type=jnp.float32) - jnp.dot(imag_in, weight_mode[1], preferred_element_type=jnp.float32)
        imag_out = jnp.dot(real_in, weight_mode[1], preferred_element_type=jnp.float32) + jnp.dot(imag_in, weight_mode[0], preferred_element_type=jnp.float32)
        return jnp.concatenate([real_out, imag_out], -1).astype(jnp.bfloat16)
    mixed_spec = lax.map(mix_one, (spectrum, weights))
    row_major = mixed_spec.reshape(M, NLAT, 2, C).transpose(1, 3, 0, 2).reshape(NLAT * C, 2 * M)
    waves = jnp.dot(row_major, synthesis, preferred_element_type=jnp.float32)
    return waves.reshape(NLAT, C, NOUT).transpose(0, 2, 1).astype(jnp.bfloat16)
```

```python
import math

import jax
import jax.numpy as jnp
from jax import lax
from jax.sharding import PartitionSpec as P

NLON = 1440
M = 512


def analysis_table(lon_index):
    mode_index = jnp.arange(M, dtype=jnp.int32)
    norm_scale = 1.0 / math.sqrt(NLON)
    phase_index = mode_index[:, None] * lon_index[None, :] % NLON
    angles = 2.0 * math.pi / NLON * phase_index.astype(jnp.float32)
    table = jnp.stack([jnp.cos(angles) * norm_scale, -jnp.sin(angles) * norm_scale], 1)
    return table.reshape(2 * M, lon_index.shape[0]).astype(jnp.bfloat16)


def synthesis_table(out_index):
    mode_index = jnp.arange(M, dtype=jnp.int32)
    norm_scale = 1.0 / math.sqrt(NLON)
    phase_out = mode_index[:, None] * out_index[None, :] % (2 * NLON)
    angles_out = 2.0 * math.pi / (2 * NLON) * phase_out.astype(jnp.float32)
    factor = jnp.where(mode_index == 0, 1.0, 2.0).astype(jnp.float32)[:, None] * norm_scale
    table = jnp.stack([jnp.cos(angles_out) * factor, -jnp.sin(angles_out) * factor], 1)
    return table.reshape(2 * M, out_index.shape[0]).astype(jnp.bfloat16)


def mix_modes(slab_modes, portion):
    re_part = portion[:, 0]
    im_part = portion[:, 1]
    wide_weight = jnp.stack(
        [jnp.concatenate([re_part, im_part], -1), jnp.concatenate([-im_part, re_part], -1)], 1
    )
    return jnp.einsum(
        "mplc,mpcd->mld", slab_modes, wide_weight, preferred_element_type=jnp.float32
    ).astype(jnp.bfloat16)


def on_device(grid_field, weights):
    lat_rows, lon_dev, channels = grid_field.shape
    lon_count = lax.axis_size("lon")
    lon_rank = lax.axis_index("lon")
    modes_dev = M // lon_count
    lon_index = lon_rank * lon_dev + jnp.arange(lon_dev, dtype=jnp.int32)
    fwd_local = analysis_table(lon_index)
    table_rows = fwd_local
    summed = lax.psum_scatter(
        jnp.einsum(
            "kn,lnc->klc", table_rows, grid_field, preferred_element_type=jnp.float32
        ).astype(jnp.bfloat16),
        "lon",
        scatter_dimension=0,
        tiled=True,
    )
    lat_count = lax.axis_size("lat")
    own_modes = modes_dev // lat_count
    moved = lax.all_to_all(
        summed.reshape(lat_count, 2 * own_modes, lat_rows, channels), "lat", 0, 0, tiled=True
    )
    spectrum = (
        moved.reshape(lat_count, own_modes, 2, lat_rows, channels)
        .transpose(1, 2, 0, 3, 4)
        .reshape(own_modes, 2, lat_count * lat_rows, channels)
    )
    mixed_own = mix_modes(spectrum, weights)
    back = mixed_own.reshape(own_modes, lat_count, lat_rows, 2 * channels).transpose(1, 0, 2, 3)
    mixed_spec = lax.all_to_all(back, "lat", 0, 0, tiled=True).reshape(
        modes_dev, lat_rows, 2 * channels
    )
    out_dev = 2 * NLON // lon_count
    out_index = lon_rank * out_dev + jnp.arange(out_dev, dtype=jnp.int32)
    inv_local = synthesis_table(out_index).reshape(M, 2, out_dev)
    portion = lax.all_gather(mixed_spec, "lon", axis=0, tiled=True)
    count = portion.shape[0]
    table_rows = inv_local
    parted = portion.reshape(count, lat_rows, 2, channels)
    running = jnp.einsum("mlpc,mpn->lnc", parted, table_rows, preferred_element_type=jnp.float32)
    return running.astype(jnp.bfloat16)


def solution(mesh):
    placed = (P(("grp", "lat"), "lon", None), P(("lon", "lat"), None, None, None))
    return jax.shard_map(
        on_device,
        mesh=mesh,
        in_specs=placed,
        out_specs=P(("grp", "lat"), "lon", None),
        check_vma=False,
    )
```

```python
import math

import jax
import jax.numpy as jnp
import numpy as np
from jax import lax
from jax.experimental import pallas as pl
from jax.experimental.pallas import tpu as pltpu
from jax.sharding import PartitionSpec as P

NLON = 1440
M = 512
ROWS = 16
HALVES = 2


def analysis_table(lon_index):
    mode_index = jnp.arange(M, dtype=jnp.int32)
    norm_scale = 1.0 / math.sqrt(NLON)
    phase_index = mode_index[:, None] * lon_index[None, :] % NLON
    angles = 2.0 * math.pi / NLON * phase_index.astype(jnp.float32)
    table = jnp.stack([jnp.cos(angles) * norm_scale, -jnp.sin(angles) * norm_scale], 1)
    return table.reshape(2 * M, lon_index.shape[0]).astype(jnp.bfloat16)


def synthesis_table(out_index):
    mode_index = jnp.arange(M, dtype=jnp.int32)
    norm_scale = 1.0 / math.sqrt(NLON)
    phase_out = mode_index[:, None] * out_index[None, :] % (2 * NLON)
    angles_out = 2.0 * math.pi / (2 * NLON) * phase_out.astype(jnp.float32)
    factor = jnp.where(mode_index == 0, 1.0, 2.0).astype(jnp.float32)[:, None] * norm_scale
    table = jnp.stack([jnp.cos(angles_out) * factor, -jnp.sin(angles_out) * factor], 1)
    return table.reshape(2 * M, out_index.shape[0]).astype(jnp.bfloat16)


def mix_modes(slab_modes, portion):
    re_part = portion[:, 0]
    im_part = portion[:, 1]
    wide_weight = jnp.stack(
        [jnp.concatenate([re_part, im_part], -1), jnp.concatenate([-im_part, re_part], -1)], 1
    )
    return jnp.einsum(
        "mplc,mpcd->mld", slab_modes, wide_weight, preferred_element_type=jnp.float32
    ).astype(jnp.bfloat16)


def on_device(grid_field, weights):
    lat_rows, lon_dev, channels = grid_field.shape
    lon_count = lax.axis_size("lon")
    lon_rank = lax.axis_index("lon")
    modes_dev = M // lon_count
    lon_index = lon_rank * lon_dev + jnp.arange(lon_dev, dtype=jnp.int32)
    summed = lax.psum_scatter(
        jnp.einsum(
            "kn,lnc->klc",
            analysis_table(lon_index),
            grid_field,
            preferred_element_type=jnp.float32,
        ).astype(jnp.bfloat16),
        "lon",
        scatter_dimension=0,
        tiled=True,
    )
    lat_count = lax.axis_size("lat")
    own_modes = modes_dev // lat_count
    moved = lax.all_to_all(
        summed.reshape(lat_count, 2 * own_modes, lat_rows, channels), "lat", 0, 0, tiled=True
    )
    spectrum = (
        moved.reshape(lat_count, own_modes, 2, lat_rows, channels)
        .transpose(1, 2, 0, 3, 4)
        .reshape(own_modes, 2, lat_count * lat_rows, channels)
    )
    mixed_own = mix_modes(spectrum, weights)
    back = mixed_own.reshape(own_modes, lat_count, lat_rows, 2 * channels).transpose(1, 0, 2, 3)
    mixed_spec = lax.all_to_all(back, "lat", 0, 0, tiled=True).reshape(
        modes_dev, lat_rows, 2 * channels
    )
    out_dev = 2 * NLON // lon_count
    out_index = lon_rank * out_dev + jnp.arange(out_dev, dtype=jnp.int32)
    inv_local = synthesis_table(out_index).reshape(M, 2, out_dev)
    portion = lax.all_gather(mixed_spec, "lon", axis=0, tiled=True)
    count = portion.shape[0]
    parted = portion.reshape(count, lat_rows, 2, channels)
    running = jnp.einsum("mlpc,mpn->lnc", parted, inv_local, preferred_element_type=jnp.float32)
    return running.astype(jnp.bfloat16)


def host_tables(lon_count, lat_count, chunks):
    mode = np.arange(M, dtype=np.int32)[:, None]
    scale = 1.0 / math.sqrt(NLON)
    turn = np.float32(2.0 * math.pi / NLON)
    angle = turn * (mode * np.arange(NLON, dtype=np.int32)[None] % NLON).astype(np.float32)
    ana = np.stack([np.cos(angle) * scale, -np.sin(angle) * scale], 1)
    ana = ana.reshape(lon_count, lat_count, chunks, ROWS, lon_count, NLON // lon_count)
    ana = ana.transpose(4, 0, 2, 1, 3, 5).reshape(
        lon_count, lon_count, chunks, lat_count * ROWS, NLON // lon_count
    )
    turn = np.float32(2.0 * math.pi / (2 * NLON))
    angle = turn * (mode * np.arange(2 * NLON, dtype=np.int32)[None] % (2 * NLON)).astype(np.float32)
    factor = np.where(mode == 0, 1.0, 2.0).astype(np.float32) * np.float32(scale)
    syn = np.stack([np.cos(angle) * factor, -np.sin(angle) * factor], 1)
    syn = syn.reshape(lon_count, lat_count, chunks, ROWS, lon_count, 2 * NLON // lon_count)
    syn = syn.transpose(4, 5, 2, 0, 1, 3).reshape(lon_count, 2 * NLON // lon_count, 2 * M)
    kind = jnp.bfloat16
    return ana.astype(np.float32).astype(kind), syn.astype(np.float32).astype(kind)


def spectral_kernel(
    lats, lat_n, chunks,
    grid_in, w_in, tab_in, full,
    g_own, g_peer, w_buf, tab, xs, acc, xr, zr, ys, xt, yt,
    local_sem, place_sem, gs, gr, x_s, x_r, z_s, z_r, y_s, y_r, a_s, a_r, b_s, b_r, f_s, f_r,
):
    lon = lax.axis_index("lon")
    z = lax.axis_index("lat")
    core = lon % 2
    side = lon // 2
    x_lon = (1 - side) * 2 + core
    mate_lon = side * 2 + 1 - core
    x_peer = {"lon": x_lon}
    mate = {"lon": mate_lon}
    mesh_id = pl.DeviceIdType.MESH
    part = lats // HALVES

    def far(src, dst, send, recv, peer):
        return pltpu.make_async_remote_copy(
            src_ref=src, dst_ref=dst, send_sem=send, recv_sem=recv,
            device_id=peer, device_id_type=mesh_id,
        )

    loads = []
    for i, block in enumerate((lon, mate_lon)):
        for j, owner in enumerate((x_lon, lon)):
            loads.append(
                pltpu.make_async_copy(
                    tab_in.at[block, owner], tab.at[i, j], local_sem.at[2 * i + j]
                )
            )
    loads.append(pltpu.make_async_copy(grid_in, g_own, local_sem.at[4]))
    w_load = pltpu.make_async_copy(w_in, w_buf, local_sem.at[5])
    for copy in loads:
        copy.start()

    barrier = pltpu.get_barrier_semaphore()
    for peer in [mate, x_peer] + [{"lat": (z + d) % lat_n} for d in range(1, lat_n)]:
        pl.semaphore_signal(barrier, inc=1, device_id=peer, device_id_type=mesh_id)
    pl.semaphore_wait(barrier, 1 + lat_n)

    g_copy = [
        far(grid_in.at[pl.ds(h * part, part)], g_peer.at[pl.ds(h * part, part)], gs.at[h], gr.at[h], mate)
        for h in range(HALVES)
    ]
    for copy in g_copy:
        copy.start()
    w_load.start()
    for copy in loads:
        copy.wait()

    def half(ref, k, h):
        return ref.at[k, :, pl.ds(h * part, part)]

    def x_copy(k, h):
        return far(half(xs, k, h), half(xr, k, h), x_s.at[k, h], x_r.at[k, h], x_peer)

    def analyse(k):
        for h in range(HALVES):
            if k == 0:
                g_copy[h].wait_recv()

            @pl.loop(h * part, (h + 1) * part)
            def _(l):
                for j, out in ((0, xs), (1, acc)):
                    value = jnp.dot(tab[0, j, k], g_own[l], preferred_element_type=jnp.float32)
                    value += jnp.dot(tab[1, j, k], g_peer[l], preferred_element_type=jnp.float32)
                    value = value.astype(jnp.bfloat16)
                    for owner in range(lat_n):
                        out[k, owner, l] = value[owner * ROWS:(owner + 1) * ROWS]

            x_copy(k, h).start()

    def z_copy(k, h, d, sending):
        source = z if sending else (z - d + lat_n) % lat_n
        target = (z + d) % lat_n if sending else z
        return far(
            acc.at[k, target, pl.ds(h * part, part)],
            zr.at[k, pl.ds(source * lats + h * part, part)],
            z_s.at[k, h, d - 1], z_r.at[k, h, d - 1], {"lat": (z + d) % lat_n},
        )

    def add_up(k):
        for h in range(HALVES):
            x_copy(k, h).wait_recv()

            @pl.loop(h * part, (h + 1) * part)
            def _(l):
                for owner in range(lat_n):
                    value = acc[k, owner, l].astype(jnp.float32) + xr[k, owner, l].astype(jnp.float32)
                    acc[k, owner, l] = value.astype(jnp.bfloat16)

            for d in range(1, lat_n):
                z_copy(k, h, d, True).start()

            @pl.loop(0, part)
            def _(l):
                zr[k, z * lats + h * part + l] = acc[k, z, h * part + l]

    def y_copy(k, d, sending):
        source = z if sending else (z - d + lat_n) % lat_n
        target = (z + d) % lat_n if sending else z
        return far(
            ys.at[k, pl.ds(target * lats, lats)],
            full.at[:, pl.ds((k * 4 + lon) * lat_n * ROWS + source * ROWS, ROWS)],
            y_s.at[k, d - 1], y_r.at[k, d - 1], {"lat": (z + d) % lat_n},
        )

    def place(k):
        return pltpu.make_async_copy(
            ys.at[k, pl.ds(z * lats, lats)],
            full.at[:, pl.ds((k * 4 + lon) * lat_n * ROWS + z * ROWS, ROWS)],
            place_sem.at[k],
        )

    tiles = lat_n * lats // 16

    def mix(k):
        for h in range(HALVES):
            for d in range(1, lat_n):
                z_copy(k, h, d, False).wait_recv()
        if k == 0:
            w_load.wait()

        @pl.loop(0, tiles)
        def _(t):
            start = pl.multiple_of(t * 16, 16)
            value = zr[k, pl.ds(start, 16)].astype(jnp.float32)
            xt[:, pl.ds(start, 16)] = jnp.swapaxes(value, 0, 1).astype(jnp.bfloat16)

        rows = lat_n * lats

        @pl.loop(0, ROWS // 2)
        def _(i):
            both = xt[pl.ds(2 * i, 2)].reshape(2 * rows, xt.shape[-1])
            by_re = jnp.dot(both, w_buf[k * (ROWS // 2) + i, 0], preferred_element_type=jnp.float32)
            by_im = jnp.dot(both, w_buf[k * (ROWS // 2) + i, 1], preferred_element_type=jnp.float32)
            yt[2 * i] = (by_re[:rows] - by_im[rows:]).astype(jnp.bfloat16)
            yt[2 * i + 1] = (by_im[:rows] + by_re[rows:]).astype(jnp.bfloat16)

        @pl.loop(0, tiles)
        def _(t):
            start = pl.multiple_of(t * 16, 16)
            value = yt[:, pl.ds(start, 16)].astype(jnp.float32)
            ys[k, pl.ds(start, 16)] = jnp.swapaxes(value, 0, 1).astype(jnp.bfloat16)

        for d in range(1, lat_n):
            y_copy(k, d, True).start()
        place(k).start()

    def block(k, owner):
        return full.at[:, pl.ds((k * 4 + owner) * lat_n * ROWS, lat_n * ROWS)]

    def across(k, sending):
        at = block(k, lon if sending else x_lon)
        return far(at, at, a_s.at[k], a_r.at[k], x_peer)

    def beside(k, sending):
        at = block(k, lon if sending else mate_lon)
        return far(at, at, b_s.at[k], b_r.at[k], mate)

    def onward(k, sending):
        at = block(k, x_lon if sending else 3 - lon)
        return far(at, at, f_s.at[k], f_r.at[k], mate)

    def spread(k):
        for d in range(1, lat_n):
            y_copy(k, d, False).wait_recv()
        place(k).wait()
        across(k, True).start()
        beside(k, True).start()

    def forward(k):
        across(k, False).wait_recv()
        onward(k, True).start()

    steps = []
    for k in range(chunks):
        steps += [(2 * k, 0, analyse, k), (2 * k + 3, 1, add_up, k), (2 * k + 6, 2, mix, k)]
        steps += [(2 * k + 9, 3, spread, k), (2 * k + 12, 4, forward, k)]
    for _, _, stage, k in sorted(steps, key=lambda s: (s[0], -s[1])):
        stage(k)

    for h in range(HALVES):
        g_copy[h].wait_send()
    for k in range(chunks):
        for h in range(HALVES):
            x_copy(k, h).wait_send()
            for d in range(1, lat_n):
                z_copy(k, h, d, True).wait_send()
        for d in range(1, lat_n):
            y_copy(k, d, True).wait_send()
        across(k, True).wait_send()
        beside(k, True).wait_send()
        beside(k, False).wait_recv()
        onward(k, True).wait_send()
        onward(k, False).wait_recv()


def synthesis_kernel(table, spectrum, out):
    out[0] = jnp.dot(table[...], spectrum[0], preferred_element_type=jnp.float32).astype(out.dtype)


def fast_device(grid_field, weights, ana, syn):
    lats, lon_dev, channels = grid_field.shape
    lat_n = lax.axis_size("lat")
    modes = weights.shape[0]
    chunks = 2 * modes // ROWS
    kind = jnp.bfloat16
    dma = pltpu.SemaphoreType.DMA
    chunk = pltpu.VMEM((chunks, lat_n, lats, ROWS, channels), kind)
    owned = pltpu.VMEM((chunks, lat_n * lats, ROWS, channels), kind)
    turned = pltpu.VMEM((ROWS, lat_n * lats, channels), kind)
    pair = dma((chunks, HALVES))
    line = dma((chunks,))

    def kernel(*refs):
        spectral_kernel(lats, lat_n, chunks, *refs)

    full = pl.pallas_call(
        kernel,
        out_shape=jax.ShapeDtypeStruct((lats, 2 * M, channels), kind),
        in_specs=[pl.BlockSpec(memory_space=pl.ANY)] * 3,
        out_specs=pl.BlockSpec(memory_space=pl.ANY),
        scratch_shapes=[
            pltpu.VMEM((lats, lon_dev, channels), kind),
            pltpu.VMEM((lats, lon_dev, channels), kind),
            pltpu.VMEM(weights.shape, kind),
            pltpu.VMEM((2, 2) + ana.shape[2:], kind),
            chunk, chunk, chunk, owned, owned, turned, turned,
            dma((6,)), line, dma((HALVES,)), dma((HALVES,)),
            pair, pair,
            dma((chunks, HALVES, lat_n - 1)), dma((chunks, HALVES, lat_n - 1)),
            dma((chunks, lat_n - 1)), dma((chunks, lat_n - 1)),
            line, line, line, line, line, line,
        ],
        compiler_params=pltpu.CompilerParams(
            collective_id=0, has_side_effects=True, vmem_limit_bytes=56 * 2**20
        ),
        cost_estimate=pl.CostEstimate(
            flops=8 * 10**9, bytes_accessed=40 * 2**20, transcendentals=0
        ),
    )(grid_field, weights, ana)
    table = lax.dynamic_index_in_dim(syn, lax.axis_index("lon"), 0, keepdims=False)
    out_dev = table.shape[0]
    return pl.pallas_call(
        synthesis_kernel,
        grid=(lats,),
        out_shape=jax.ShapeDtypeStruct((lats, out_dev, channels), kind),
        in_specs=[
            pl.BlockSpec(table.shape, lambda l: (0, 0)),
            pl.BlockSpec((1, 2 * M, channels), lambda l: (l, 0, 0)),
        ],
        out_specs=pl.BlockSpec((1, out_dev, channels), lambda l: (l, 0, 0)),
        compiler_params=pltpu.CompilerParams(vmem_limit_bytes=40 * 2**20),
    )(table, full)


def solution(mesh):
    placed = (P(("grp", "lat"), "lon", None), P(("lon", "lat"), None, None, None))
    lon_count, lat_count = mesh.shape["lon"], mesh.shape["lat"]
    owned_rows = 2 * M // (lon_count * lat_count)
    body = on_device
    if lon_count == 4 and lat_count == 4 and owned_rows % ROWS == 0:
        ana, syn = host_tables(lon_count, lat_count, owned_rows // ROWS)

        def body(grid_field, weights):
            return fast_device(grid_field, weights, jnp.asarray(ana), jnp.asarray(syn))

    return jax.shard_map(
        body,
        mesh=mesh,
        in_specs=placed,
        out_specs=P(("grp", "lat"), "lon", None),
        check_vma=False,
    )
```

```python
import math

import jax
import jax.numpy as jnp
import numpy as np
from jax import lax
from jax.experimental import pallas as pl
from jax.experimental.pallas import tpu as pltpu
from jax.sharding import PartitionSpec as P

NLON = 1440
M = 512
ROWS = 16
PIECES = 4
BACK = 2
LATS = 4


def analysis_table(lon_index):
    mode_index = jnp.arange(M, dtype=jnp.int32)
    norm_scale = 1.0 / math.sqrt(NLON)
    phase_index = mode_index[:, None] * lon_index[None, :] % NLON
    angles = 2.0 * math.pi / NLON * phase_index.astype(jnp.float32)
    table = jnp.stack([jnp.cos(angles) * norm_scale, -jnp.sin(angles) * norm_scale], 1)
    return table.reshape(2 * M, lon_index.shape[0]).astype(jnp.bfloat16)


def synthesis_table(out_index):
    mode_index = jnp.arange(M, dtype=jnp.int32)
    norm_scale = 1.0 / math.sqrt(NLON)
    phase_out = mode_index[:, None] * out_index[None, :] % (2 * NLON)
    angles_out = 2.0 * math.pi / (2 * NLON) * phase_out.astype(jnp.float32)
    factor = jnp.where(mode_index == 0, 1.0, 2.0).astype(jnp.float32)[:, None] * norm_scale
    table = jnp.stack([jnp.cos(angles_out) * factor, -jnp.sin(angles_out) * factor], 1)
    return table.reshape(2 * M, out_index.shape[0]).astype(jnp.bfloat16)


def mix_modes(slab_modes, portion):
    re_part = portion[:, 0]
    im_part = portion[:, 1]
    wide_weight = jnp.stack(
        [jnp.concatenate([re_part, im_part], -1), jnp.concatenate([-im_part, re_part], -1)], 1
    )
    return jnp.einsum(
        "mplc,mpcd->mld", slab_modes, wide_weight, preferred_element_type=jnp.float32
    ).astype(jnp.bfloat16)


def on_device(grid_field, weights):
    lat_rows, lon_dev, channels = grid_field.shape
    lon_count = lax.axis_size("lon")
    lon_rank = lax.axis_index("lon")
    modes_dev = M // lon_count
    lon_index = lon_rank * lon_dev + jnp.arange(lon_dev, dtype=jnp.int32)
    summed = lax.psum_scatter(
        jnp.einsum(
            "kn,lnc->klc",
            analysis_table(lon_index),
            grid_field,
            preferred_element_type=jnp.float32,
        ).astype(jnp.bfloat16),
        "lon",
        scatter_dimension=0,
        tiled=True,
    )
    lat_count = lax.axis_size("lat")
    own_modes = modes_dev // lat_count
    moved = lax.all_to_all(
        summed.reshape(lat_count, 2 * own_modes, lat_rows, channels), "lat", 0, 0, tiled=True
    )
    spectrum = (
        moved.reshape(lat_count, own_modes, 2, lat_rows, channels)
        .transpose(1, 2, 0, 3, 4)
        .reshape(own_modes, 2, lat_count * lat_rows, channels)
    )
    mixed_own = mix_modes(spectrum, weights)
    back = mixed_own.reshape(own_modes, lat_count, lat_rows, 2 * channels).transpose(1, 0, 2, 3)
    mixed_spec = lax.all_to_all(back, "lat", 0, 0, tiled=True).reshape(
        modes_dev, lat_rows, 2 * channels
    )
    out_dev = 2 * NLON // lon_count
    out_index = lon_rank * out_dev + jnp.arange(out_dev, dtype=jnp.int32)
    inv_local = synthesis_table(out_index).reshape(M, 2, out_dev)
    portion = lax.all_gather(mixed_spec, "lon", axis=0, tiled=True)
    count = portion.shape[0]
    parted = portion.reshape(count, lat_rows, 2, channels)
    running = jnp.einsum("mlpc,mpn->lnc", parted, inv_local, preferred_element_type=jnp.float32)
    return running.astype(jnp.bfloat16)


def host_tables(lon_count, lat_count, chunks):
    mode = np.arange(M, dtype=np.int32)[:, None]
    scale = 1.0 / math.sqrt(NLON)
    turn = np.float32(2.0 * math.pi / NLON)
    angle = turn * (mode * np.arange(NLON, dtype=np.int32)[None] % NLON).astype(np.float32)
    ana = np.stack([np.cos(angle) * scale, -np.sin(angle) * scale], 1)
    ana = ana.reshape(lon_count, lat_count, chunks, ROWS, lon_count, NLON // lon_count)
    ana = ana.transpose(4, 0, 2, 1, 3, 5).reshape(
        lon_count, lon_count, chunks, lat_count * ROWS, NLON // lon_count
    )
    turn = np.float32(2.0 * math.pi / (2 * NLON))
    angle = turn * (mode * np.arange(2 * NLON, dtype=np.int32)[None] % (2 * NLON)).astype(np.float32)
    factor = np.where(mode == 0, 1.0, 2.0).astype(np.float32) * np.float32(scale)
    syn = np.stack([np.cos(angle) * factor, -np.sin(angle) * factor], 1)
    syn = syn.reshape(lon_count, lat_count, chunks, ROWS, lon_count, 2 * NLON // lon_count)
    syn = syn.transpose(4, 5, 2, 0, 1, 3).reshape(lon_count, 2 * NLON // lon_count, 2, M)
    syn = syn.transpose(0, 2, 1, 3)
    kind = jnp.bfloat16
    return ana.astype(np.float32).astype(kind), syn.astype(np.float32).astype(kind)


def spectral_kernel(
    lats, lat_n, chunks,
    grid_in, w_in, tab_in, syn_in, full, early,
    syn, g_own, g_peer, w_buf, tab, xs, acc, xr, zr, ys, xt, yt,
    local_sem, place_sem, gs, gr, x_s, x_r, z_s, z_r, y_s, y_r, a_s, a_r, b_s, b_r, f_s, f_r,
):
    lon = lax.axis_index("lon")
    z = lax.axis_index("lat")
    core = lon % 2
    side = lon // 2
    x_lon = (1 - side) * 2 + core
    mate_lon = side * 2 + 1 - core
    x_peer = {"lon": x_lon}
    mate = {"lon": mate_lon}
    mesh_id = pl.DeviceIdType.MESH
    part = lats // PIECES

    def far(src, dst, send, recv, peer):
        return pltpu.make_async_remote_copy(
            src_ref=src, dst_ref=dst, send_sem=send, recv_sem=recv,
            device_id=peer, device_id_type=mesh_id,
        )

    loads = []
    for i, block in enumerate((lon, mate_lon)):
        for j, owner in enumerate((x_lon, lon)):
            loads.append(
                pltpu.make_async_copy(
                    tab_in.at[block, owner], tab.at[i, :, j], local_sem.at[2 * i + j]
                )
            )
    loads.append(pltpu.make_async_copy(grid_in, g_own, local_sem.at[4]))
    w_load = pltpu.make_async_copy(w_in, w_buf, local_sem.at[5])
    syn_load = pltpu.make_async_copy(syn_in.at[lon, 0], syn, local_sem.at[6])
    for copy in loads:
        copy.start()

    barrier = pltpu.get_barrier_semaphore()
    for peer in [mate, x_peer] + [{"lat": (z + d) % lat_n} for d in range(1, lat_n)]:
        pl.semaphore_signal(barrier, inc=1, device_id=peer, device_id_type=mesh_id)
    pl.semaphore_wait(barrier, 1 + lat_n)

    g_copy = [
        far(grid_in.at[pl.ds(h * part, part)], g_peer.at[pl.ds(h * part, part)], gs.at[h], gr.at[h], mate)
        for h in range(PIECES)
    ]
    for copy in g_copy:
        copy.start()
    w_load.start()
    syn_load.start()
    for copy in loads:
        copy.wait()

    def half(ref, k, h):
        return ref.at[k, :, pl.ds(h * part, part)]

    def x_copy(k, h):
        return far(half(xs, k, h), half(xr, k, h), x_s.at[k, h], x_r.at[k, h], x_peer)

    def analyse(k):
        for h in range(PIECES):
            if k == 0:
                g_copy[h].wait_recv()

            @pl.loop(h * part, (h + 1) * part)
            def _(l):
                wide = (2 * lat_n * ROWS, tab.shape[-1])
                value = jnp.dot(
                    tab[0, k].reshape(wide), g_own[l], preferred_element_type=jnp.float32
                )
                value += jnp.dot(
                    tab[1, k].reshape(wide), g_peer[l], preferred_element_type=jnp.float32
                )
                value = value.astype(jnp.bfloat16)
                for j, out in ((0, xs), (1, acc)):
                    for owner in range(lat_n):
                        first = (j * lat_n + owner) * ROWS
                        out[k, owner, l] = value[first:first + ROWS]

            x_copy(k, h).start()

    def z_copy(k, h, d, sending):
        source = z if sending else (z - d + lat_n) % lat_n
        target = (z + d) % lat_n if sending else z
        return far(
            acc.at[k, target, pl.ds(h * part, part)],
            zr.at[k, pl.ds(source * lats + h * part, part)],
            z_s.at[k, h, d - 1], z_r.at[k, h, d - 1], {"lat": (z + d) % lat_n},
        )

    def add_up(k):
        for h in range(PIECES):
            x_copy(k, h).wait_recv()

            @pl.loop(h * part, (h + 1) * part)
            def _(l):
                for owner in range(lat_n):
                    value = acc[k, owner, l].astype(jnp.float32) + xr[k, owner, l].astype(jnp.float32)
                    acc[k, owner, l] = value.astype(jnp.bfloat16)

            for d in range(1, lat_n):
                z_copy(k, h, d, True).start()

            @pl.loop(0, part)
            def _(l):
                zr[k, z * lats + h * part + l] = acc[k, z, h * part + l]

    some = lats // BACK

    def rows_of(k, owner, source, h):
        first = (k * 4 + owner) * lat_n * ROWS + source * ROWS
        return full.at[pl.ds(h * some, some), pl.ds(first, ROWS)]

    def y_copy(k, h, d, sending):
        source = z if sending else (z - d + lat_n) % lat_n
        target = (z + d) % lat_n if sending else z
        return far(
            ys.at[k, pl.ds(target * lats + h * some, some)],
            rows_of(k, lon, source, h),
            y_s.at[k, h, d - 1], y_r.at[k, h, d - 1], {"lat": (z + d) % lat_n},
        )

    def place(k, h):
        return pltpu.make_async_copy(
            ys.at[k, pl.ds(z * lats + h * some, some)],
            rows_of(k, lon, z, h),
            place_sem.at[k, h],
        )

    tiles = lat_n * lats // 16

    def mix(k):
        for h in range(PIECES):
            for d in range(1, lat_n):
                z_copy(k, h, d, False).wait_recv()
        if k == 0:
            w_load.wait()

        @pl.loop(0, tiles)
        def _(t):
            start = pl.multiple_of(t * 16, 16)
            value = zr[k, pl.ds(start, 16)].astype(jnp.float32)
            xt[:, pl.ds(start, 16)] = jnp.swapaxes(value, 0, 1).astype(jnp.bfloat16)

        rows = lat_n * lats

        @pl.loop(0, ROWS // 2)
        def _(i):
            both = xt[pl.ds(2 * i, 2)].reshape(2 * rows, xt.shape[-1])
            by_re = jnp.dot(both, w_buf[k * (ROWS // 2) + i, 0], preferred_element_type=jnp.float32)
            by_im = jnp.dot(both, w_buf[k * (ROWS // 2) + i, 1], preferred_element_type=jnp.float32)
            yt[2 * i] = (by_re[:rows] - by_im[rows:]).astype(jnp.bfloat16)
            yt[2 * i + 1] = (by_im[:rows] + by_re[rows:]).astype(jnp.bfloat16)

        @pl.loop(0, tiles)
        def _(t):
            start = pl.multiple_of(t * 16, 16)
            value = yt[:, pl.ds(start, 16)].astype(jnp.float32)
            ys[k, pl.ds(start, 16)] = jnp.swapaxes(value, 0, 1).astype(jnp.bfloat16)

        for h in range(BACK):
            for d in range(1, lat_n):
                y_copy(k, h, d, True).start()
            place(k, h).start()

    def block(k, h, owner):
        first = (k * 4 + owner) * lat_n * ROWS
        return full.at[pl.ds(h * some, some), pl.ds(first, lat_n * ROWS)]

    def across(k, h, sending):
        at = block(k, h, lon if sending else x_lon)
        return far(at, at, a_s.at[k, h], a_r.at[k, h], x_peer)

    def beside(k, h, sending):
        at = block(k, h, lon if sending else mate_lon)
        return far(at, at, b_s.at[k, h], b_r.at[k, h], mate)

    def onward(k, h, sending):
        at = block(k, h, x_lon if sending else 3 - lon)
        return far(at, at, f_s.at[k, h], f_r.at[k, h], mate)

    def spread(k, h):
        for d in range(1, lat_n):
            y_copy(k, h, d, False).wait_recv()
        place(k, h).wait()
        across(k, h, True).start()
        beside(k, h, True).start()

    def forward(k, h):
        across(k, h, False).wait_recv()
        onward(k, h, True).start()

    def arrived(k):
        for h in range(BACK):
            beside(k, h, False).wait_recv()
            onward(k, h, False).wait_recv()

    def spread_all(k):
        for h in range(BACK):
            spread(k, h)

    def forward_all(k):
        for h in range(BACK):
            forward(k, h)

    def first_sum(part_of):
        if part_of == 0:
            arrived(0)
            arrived(1)
            syn_load.wait()
        steps = lats // LATS // 2

        def body(spectrum, out):
            for i in range(LATS):
                value = jnp.dot(syn[...], spectrum[i], preferred_element_type=jnp.float32)
                out[i] = value.astype(out.dtype)

        pltpu.emit_pipeline(
            body,
            grid=(steps,),
            in_specs=[pl.BlockSpec((LATS, M, full.shape[2]), lambda l: (l + part_of * steps, 0, 0))],
            out_specs=[pl.BlockSpec((LATS,) + early.shape[1:], lambda l: (l + part_of * steps, 0, 0))],
        )(full, early)

    analyse(0)
    analyse(1)
    add_up(0)
    analyse(2)
    add_up(1)
    analyse(3)
    mix(0)
    add_up(2)
    mix(1)
    spread_all(0)
    add_up(3)
    mix(2)
    spread_all(1)
    forward_all(0)
    mix(3)
    forward_all(1)
    first_sum(0)
    spread(2, 0)
    first_sum(1)
    for h in range(1, BACK):
        spread(2, h)
    for h in range(BACK):
        spread(3, h)
        forward(2, h)
    forward_all(3)

    for h in range(PIECES):
        g_copy[h].wait_send()
    for k in range(chunks):
        for h in range(PIECES):
            x_copy(k, h).wait_send()
            for d in range(1, lat_n):
                z_copy(k, h, d, True).wait_send()
        for h in range(BACK):
            for d in range(1, lat_n):
                y_copy(k, h, d, True).wait_send()
            across(k, h, True).wait_send()
            beside(k, h, True).wait_send()
            onward(k, h, True).wait_send()
    arrived(2)
    arrived(3)


def synthesis_kernel(rank, table, spectrum, early, out):
    for i in range(LATS):
        value = jnp.dot(table[0, 0], spectrum[i], preferred_element_type=jnp.float32)
        out[i] = (value + early[i].astype(jnp.float32)).astype(out.dtype)


def fast_device(grid_field, weights, ana, syn):
    lats, lon_dev, channels = grid_field.shape
    lat_n = lax.axis_size("lat")
    modes = weights.shape[0]
    chunks = 2 * modes // ROWS
    kind = jnp.bfloat16
    dma = pltpu.SemaphoreType.DMA
    chunk = pltpu.VMEM((chunks, lat_n, lats, ROWS, channels), kind)
    owned = pltpu.VMEM((chunks, lat_n * lats, ROWS, channels), kind)
    turned = pltpu.VMEM((ROWS, lat_n * lats, channels), kind)
    pair = dma((chunks, PIECES))

    def kernel(*refs):
        spectral_kernel(lats, lat_n, chunks, *refs)

    out_dev = syn.shape[2]
    back = dma((chunks, BACK))
    full, early = pl.pallas_call(
        kernel,
        out_shape=[
            jax.ShapeDtypeStruct((lats, 2 * M, channels), kind),
            jax.ShapeDtypeStruct((lats, out_dev, channels), kind),
        ],
        in_specs=[pl.BlockSpec(memory_space=pl.ANY)] * 4,
        out_specs=[pl.BlockSpec(memory_space=pl.ANY)] * 2,
        scratch_shapes=[
            pltpu.VMEM((out_dev, M), kind),
            pltpu.VMEM((lats, lon_dev, channels), kind),
            pltpu.VMEM((lats, lon_dev, channels), kind),
            pltpu.VMEM(weights.shape, kind),
            pltpu.VMEM((2, chunks, 2) + ana.shape[3:], kind),
            chunk, chunk, chunk, owned, owned, turned, turned,
            dma((7,)), back, dma((PIECES,)), dma((PIECES,)),
            pair, pair,
            dma((chunks, PIECES, lat_n - 1)), dma((chunks, PIECES, lat_n - 1)),
            dma((chunks, BACK, lat_n - 1)), dma((chunks, BACK, lat_n - 1)),
            back, back, back, back, back, back,
        ],
        compiler_params=pltpu.CompilerParams(
            collective_id=0, has_side_effects=True, vmem_limit_bytes=56 * 2**20
        ),
        cost_estimate=pl.CostEstimate(
            flops=12 * 10**9, bytes_accessed=60 * 2**20, transcendentals=0
        ),
    )(grid_field, weights, ana, syn)
    rank = lax.axis_index("lon").astype(jnp.int32).reshape(1)
    return pl.pallas_call(
        synthesis_kernel,
        grid_spec=pltpu.PrefetchScalarGridSpec(
            num_scalar_prefetch=1,
            grid=(lats // LATS,),
            in_specs=[
                pl.BlockSpec((1, 1, out_dev, M), lambda l, r: (r[0], 1, 0, 0)),
                pl.BlockSpec((LATS, M, channels), lambda l, r: (l, 1, 0)),
                pl.BlockSpec((LATS, out_dev, channels), lambda l, r: (l, 0, 0)),
            ],
            out_specs=pl.BlockSpec((LATS, out_dev, channels), lambda l, r: (l, 0, 0)),
        ),
        out_shape=jax.ShapeDtypeStruct((lats, out_dev, channels), kind),
        compiler_params=pltpu.CompilerParams(vmem_limit_bytes=60 * 2**20),
    )(rank, syn, full, early)


def solution(mesh):
    placed = (P(("grp", "lat"), "lon", None), P(("lon", "lat"), None, None, None))
    lon_count, lat_count = mesh.shape["lon"], mesh.shape["lat"]
    owned_rows = 2 * M // (lon_count * lat_count)
    body = on_device
    if lon_count == 4 and lat_count == 4 and owned_rows % ROWS == 0:
        ana, syn = host_tables(lon_count, lat_count, owned_rows // ROWS)

        def body(grid_field, weights):
            return fast_device(grid_field, weights, jnp.asarray(ana), jnp.asarray(syn))

    return jax.shard_map(
        body,
        mesh=mesh,
        in_specs=placed,
        out_specs=P(("grp", "lat"), "lon", None),
        check_vma=False,
    )
```

```python
import math

import jax
import jax.numpy as jnp
import numpy as np
from jax import lax
from jax.experimental import pallas as pl
from jax.experimental.pallas import tpu as pltpu
from jax.sharding import PartitionSpec as P

NLON = 1440
M = 512
ROWS = 16
PIECES = 4
BACK = 2
LAST = 6
LATS = 4


def analysis_table(lon_index):
    mode_index = jnp.arange(M, dtype=jnp.int32)
    norm_scale = 1.0 / math.sqrt(NLON)
    phase_index = mode_index[:, None] * lon_index[None, :] % NLON
    angles = 2.0 * math.pi / NLON * phase_index.astype(jnp.float32)
    table = jnp.stack([jnp.cos(angles) * norm_scale, -jnp.sin(angles) * norm_scale], 1)
    return table.reshape(2 * M, lon_index.shape[0]).astype(jnp.bfloat16)


def synthesis_table(out_index):
    mode_index = jnp.arange(M, dtype=jnp.int32)
    norm_scale = 1.0 / math.sqrt(NLON)
    phase_out = mode_index[:, None] * out_index[None, :] % (2 * NLON)
    angles_out = 2.0 * math.pi / (2 * NLON) * phase_out.astype(jnp.float32)
    factor = jnp.where(mode_index == 0, 1.0, 2.0).astype(jnp.float32)[:, None] * norm_scale
    table = jnp.stack([jnp.cos(angles_out) * factor, -jnp.sin(angles_out) * factor], 1)
    return table.reshape(2 * M, out_index.shape[0]).astype(jnp.bfloat16)


def mix_modes(slab_modes, portion):
    re_part = portion[:, 0]
    im_part = portion[:, 1]
    wide_weight = jnp.stack(
        [jnp.concatenate([re_part, im_part], -1), jnp.concatenate([-im_part, re_part], -1)], 1
    )
    return jnp.einsum(
        "mplc,mpcd->mld", slab_modes, wide_weight, preferred_element_type=jnp.float32
    ).astype(jnp.bfloat16)


def on_device(grid_field, weights):
    lat_rows, lon_dev, channels = grid_field.shape
    lon_count = lax.axis_size("lon")
    lon_rank = lax.axis_index("lon")
    modes_dev = M // lon_count
    lon_index = lon_rank * lon_dev + jnp.arange(lon_dev, dtype=jnp.int32)
    summed = lax.psum_scatter(
        jnp.einsum(
            "kn,lnc->klc",
            analysis_table(lon_index),
            grid_field,
            preferred_element_type=jnp.float32,
        ).astype(jnp.bfloat16),
        "lon",
        scatter_dimension=0,
        tiled=True,
    )
    lat_count = lax.axis_size("lat")
    own_modes = modes_dev // lat_count
    moved = lax.all_to_all(
        summed.reshape(lat_count, 2 * own_modes, lat_rows, channels), "lat", 0, 0, tiled=True
    )
    spectrum = (
        moved.reshape(lat_count, own_modes, 2, lat_rows, channels)
        .transpose(1, 2, 0, 3, 4)
        .reshape(own_modes, 2, lat_count * lat_rows, channels)
    )
    mixed_own = mix_modes(spectrum, weights)
    back = mixed_own.reshape(own_modes, lat_count, lat_rows, 2 * channels).transpose(1, 0, 2, 3)
    mixed_spec = lax.all_to_all(back, "lat", 0, 0, tiled=True).reshape(
        modes_dev, lat_rows, 2 * channels
    )
    out_dev = 2 * NLON // lon_count
    out_index = lon_rank * out_dev + jnp.arange(out_dev, dtype=jnp.int32)
    inv_local = synthesis_table(out_index).reshape(M, 2, out_dev)
    portion = lax.all_gather(mixed_spec, "lon", axis=0, tiled=True)
    count = portion.shape[0]
    parted = portion.reshape(count, lat_rows, 2, channels)
    running = jnp.einsum("mlpc,mpn->lnc", parted, inv_local, preferred_element_type=jnp.float32)
    return running.astype(jnp.bfloat16)


def host_tables(lon_count, lat_count, chunks):
    mode = np.arange(M, dtype=np.int32)[:, None]
    scale = 1.0 / math.sqrt(NLON)
    turn = np.float32(2.0 * math.pi / NLON)
    angle = turn * (mode * np.arange(NLON, dtype=np.int32)[None] % NLON).astype(np.float32)
    ana = np.stack([np.cos(angle) * scale, -np.sin(angle) * scale], 1)
    ana = ana.reshape(lon_count, lat_count, chunks, ROWS, lon_count, NLON // lon_count)
    ana = ana.transpose(4, 0, 2, 1, 3, 5).reshape(
        lon_count, lon_count, chunks, lat_count * ROWS, NLON // lon_count
    )
    turn = np.float32(2.0 * math.pi / (2 * NLON))
    angle = turn * (mode * np.arange(2 * NLON, dtype=np.int32)[None] % (2 * NLON)).astype(np.float32)
    factor = np.where(mode == 0, 1.0, 2.0).astype(np.float32) * np.float32(scale)
    syn = np.stack([np.cos(angle) * factor, -np.sin(angle) * factor], 1)
    syn = syn.reshape(lon_count, lat_count, chunks, ROWS, lon_count, 2 * NLON // lon_count)
    syn = syn.transpose(4, 5, 2, 0, 1, 3).reshape(lon_count, 2 * NLON // lon_count, 2, M)
    syn = syn.transpose(0, 2, 1, 3)
    kind = jnp.bfloat16
    return ana.astype(np.float32).astype(kind), syn.astype(np.float32).astype(kind)


def spectral_kernel(
    lats, lat_n, chunks,
    grid_in, w_in, tab_in, syn_in, full, early,
    syn, g_own, g_peer, w_buf, tab, xs, acc, xr, zr, ys, xt, yt,
    local_sem, place_sem, gs, gr, x_s, x_r, z_s, z_r, y_s, y_r, a_s, a_r, b_s, b_r, f_s, f_r,
):
    lon = lax.axis_index("lon")
    z = lax.axis_index("lat")
    core = lon % 2
    side = lon // 2
    x_lon = (1 - side) * 2 + core
    mate_lon = side * 2 + 1 - core
    x_peer = {"lon": x_lon}
    mate = {"lon": mate_lon}
    mesh_id = pl.DeviceIdType.MESH
    part = lats // PIECES

    def far(src, dst, send, recv, peer):
        return pltpu.make_async_remote_copy(
            src_ref=src, dst_ref=dst, send_sem=send, recv_sem=recv,
            device_id=peer, device_id_type=mesh_id,
        )

    loads = []
    for i, block in enumerate((lon, mate_lon)):
        for j, owner in enumerate((x_lon, lon)):
            loads.append(
                pltpu.make_async_copy(
                    tab_in.at[block, owner], tab.at[i, :, j], local_sem.at[2 * i + j]
                )
            )
    loads.append(pltpu.make_async_copy(grid_in, g_own, local_sem.at[4]))
    w_load = pltpu.make_async_copy(w_in, w_buf, local_sem.at[5])
    syn_load = pltpu.make_async_copy(syn_in.at[lon, 0], syn, local_sem.at[6])
    for copy in loads:
        copy.start()

    barrier = pltpu.get_barrier_semaphore()
    for peer in [mate, x_peer] + [{"lat": (z + d) % lat_n} for d in range(1, lat_n)]:
        pl.semaphore_signal(barrier, inc=1, device_id=peer, device_id_type=mesh_id)
    pl.semaphore_wait(barrier, 1 + lat_n)

    g_copy = [
        far(grid_in.at[pl.ds(h * part, part)], g_peer.at[pl.ds(h * part, part)], gs.at[h], gr.at[h], mate)
        for h in range(PIECES)
    ]
    for copy in g_copy:
        copy.start()
    w_load.start()
    syn_load.start()
    for copy in loads:
        copy.wait()

    def half(ref, k, h):
        return ref.at[k, :, pl.ds(h * part, part)]

    def x_copy(k, h):
        return far(half(xs, k, h), half(xr, k, h), x_s.at[k, h], x_r.at[k, h], x_peer)

    def analyse(k):
        for h in range(PIECES):
            if k == 0:
                g_copy[h].wait_recv()

            @pl.loop(h * part, (h + 1) * part)
            def _(l):
                wide = (2 * lat_n * ROWS, tab.shape[-1])
                value = jnp.dot(
                    tab[0, k].reshape(wide), g_own[l], preferred_element_type=jnp.float32
                )
                value += jnp.dot(
                    tab[1, k].reshape(wide), g_peer[l], preferred_element_type=jnp.float32
                )
                value = value.astype(jnp.bfloat16)
                for j, out in ((0, xs), (1, acc)):
                    for owner in range(lat_n):
                        first = (j * lat_n + owner) * ROWS
                        out[k, owner, l] = value[first:first + ROWS]

            x_copy(k, h).start()

    def z_copy(k, h, d, sending):
        source = z if sending else (z - d + lat_n) % lat_n
        target = (z + d) % lat_n if sending else z
        return far(
            acc.at[k, target, pl.ds(h * part, part)],
            zr.at[k, pl.ds(source * lats + h * part, part)],
            z_s.at[k, h, d - 1], z_r.at[k, h, d - 1], {"lat": (z + d) % lat_n},
        )

    def add_up(k):
        for h in range(PIECES):
            x_copy(k, h).wait_recv()

            @pl.loop(h * part, (h + 1) * part)
            def _(l):
                for owner in range(lat_n):
                    value = acc[k, owner, l].astype(jnp.float32) + xr[k, owner, l].astype(jnp.float32)
                    acc[k, owner, l] = value.astype(jnp.bfloat16)

            for d in range(1, lat_n):
                z_copy(k, h, d, True).start()

            @pl.loop(0, part)
            def _(l):
                zr[k, z * lats + h * part + l] = acc[k, z, h * part + l]

    some = lats // BACK

    def rows_of(k, owner, source, h):
        first = (k * 4 + owner) * lat_n * ROWS + source * ROWS
        return full.at[pl.ds(h * some, some), pl.ds(first, ROWS)]

    def y_copy(k, h, d, sending):
        source = z if sending else (z - d + lat_n) % lat_n
        target = (z + d) % lat_n if sending else z
        return far(
            ys.at[k, pl.ds(target * lats + h * some, some)],
            rows_of(k, lon, source, h),
            y_s.at[k, h, d - 1], y_r.at[k, h, d - 1], {"lat": (z + d) % lat_n},
        )

    def place(k, h):
        return pltpu.make_async_copy(
            ys.at[k, pl.ds(z * lats + h * some, some)],
            rows_of(k, lon, z, h),
            place_sem.at[k, h],
        )

    tiles = lat_n * lats // 16

    def mix(k):
        for h in range(PIECES):
            for d in range(1, lat_n):
                z_copy(k, h, d, False).wait_recv()
        if k == 0:
            w_load.wait()

        @pl.loop(0, tiles)
        def _(t):
            start = pl.multiple_of(t * 16, 16)
            value = zr[k, pl.ds(start, 16)].astype(jnp.float32)
            xt[:, pl.ds(start, 16)] = jnp.swapaxes(value, 0, 1).astype(jnp.bfloat16)

        rows = lat_n * lats

        @pl.loop(0, ROWS // 2)
        def _(i):
            both = xt[pl.ds(2 * i, 2)].reshape(2 * rows, xt.shape[-1])
            by_re = jnp.dot(both, w_buf[k * (ROWS // 2) + i, 0], preferred_element_type=jnp.float32)
            by_im = jnp.dot(both, w_buf[k * (ROWS // 2) + i, 1], preferred_element_type=jnp.float32)
            yt[2 * i] = (by_re[:rows] - by_im[rows:]).astype(jnp.bfloat16)
            yt[2 * i + 1] = (by_im[:rows] + by_re[rows:]).astype(jnp.bfloat16)

        @pl.loop(0, tiles)
        def _(t):
            start = pl.multiple_of(t * 16, 16)
            value = yt[:, pl.ds(start, 16)].astype(jnp.float32)
            ys[k, pl.ds(start, 16)] = jnp.swapaxes(value, 0, 1).astype(jnp.bfloat16)

        for h in range(BACK):
            for d in range(1, lat_n):
                y_copy(k, h, d, True).start()
            place(k, h).start()

    def block(k, h, owner):
        first = (k * 4 + owner) * lat_n * ROWS
        return full.at[pl.ds(h * some, some), pl.ds(first, lat_n * ROWS)]

    def across(k, h, sending):
        at = block(k, h, lon if sending else x_lon)
        return far(at, at, a_s.at[k, h], a_r.at[k, h], x_peer)

    def beside(k, h, sending):
        at = block(k, h, lon if sending else mate_lon)
        return far(at, at, b_s.at[k, h], b_r.at[k, h], mate)

    def onward(k, h, sending):
        at = block(k, h, x_lon if sending else 3 - lon)
        return far(at, at, f_s.at[k, h], f_r.at[k, h], mate)

    def spread(k, h):
        for d in range(1, lat_n):
            y_copy(k, h, d, False).wait_recv()
        place(k, h).wait()
        across(k, h, True).start()
        beside(k, h, True).start()

    def forward(k, h):
        across(k, h, False).wait_recv()
        onward(k, h, True).start()

    def arrived(k):
        for h in range(BACK):
            beside(k, h, False).wait_recv()
            onward(k, h, False).wait_recv()

    def spread_all(k):
        for h in range(BACK):
            spread(k, h)

    def forward_all(k):
        for h in range(BACK):
            forward(k, h)

    def first_sum(part_of):
        if part_of == 0:
            arrived(0)
            arrived(1)
            syn_load.wait()
        steps = lats // LATS // 2

        def body(spectrum, out):
            for i in range(LATS):
                value = jnp.dot(syn[...], spectrum[i], preferred_element_type=jnp.float32)
                out[i] = value.astype(out.dtype)

        pltpu.emit_pipeline(
            body,
            grid=(steps,),
            in_specs=[pl.BlockSpec((LATS, M, full.shape[2]), lambda l: (l + part_of * steps, 0, 0))],
            out_specs=[pl.BlockSpec((LATS,) + early.shape[1:], lambda l: (l + part_of * steps, 0, 0))],
        )(full, early)

    analyse(0)
    analyse(1)
    add_up(0)
    analyse(2)
    add_up(1)
    analyse(3)
    mix(0)
    add_up(2)
    mix(1)
    spread_all(0)
    add_up(3)
    mix(2)
    spread_all(1)
    forward_all(0)
    mix(3)
    forward_all(1)
    spread_all(2)
    first_sum(0)
    for h in range(BACK):
        spread(3, h)
        forward(2, h)
    first_sum(1)
    forward_all(3)

    for h in range(PIECES):
        g_copy[h].wait_send()
    for k in range(chunks):
        for h in range(PIECES):
            x_copy(k, h).wait_send()
            for d in range(1, lat_n):
                z_copy(k, h, d, True).wait_send()
        for h in range(BACK):
            for d in range(1, lat_n):
                y_copy(k, h, d, True).wait_send()
            across(k, h, True).wait_send()
            beside(k, h, True).wait_send()
            onward(k, h, True).wait_send()
    arrived(2)
    arrived(3)


def synthesis_kernel(rank, table, spectrum, early, out):
    for i in range(LAST):
        value = jnp.dot(table[0, 0], spectrum[i], preferred_element_type=jnp.float32)
        out[i] = (value + early[i].astype(jnp.float32)).astype(out.dtype)


def fast_device(grid_field, weights, ana, syn):
    lats, lon_dev, channels = grid_field.shape
    lat_n = lax.axis_size("lat")
    modes = weights.shape[0]
    chunks = 2 * modes // ROWS
    kind = jnp.bfloat16
    dma = pltpu.SemaphoreType.DMA
    chunk = pltpu.VMEM((chunks, lat_n, lats, ROWS, channels), kind)
    owned = pltpu.VMEM((chunks, lat_n * lats, ROWS, channels), kind)
    turned = pltpu.VMEM((ROWS, lat_n * lats, channels), kind)
    pair = dma((chunks, PIECES))

    def kernel(*refs):
        spectral_kernel(lats, lat_n, chunks, *refs)

    out_dev = syn.shape[2]
    back = dma((chunks, BACK))
    full, early = pl.pallas_call(
        kernel,
        out_shape=[
            jax.ShapeDtypeStruct((lats, 2 * M, channels), kind),
            jax.ShapeDtypeStruct((lats, out_dev, channels), kind),
        ],
        in_specs=[pl.BlockSpec(memory_space=pl.ANY)] * 4,
        out_specs=[pl.BlockSpec(memory_space=pl.ANY)] * 2,
        scratch_shapes=[
            pltpu.VMEM((out_dev, M), kind),
            pltpu.VMEM((lats, lon_dev, channels), kind),
            pltpu.VMEM((lats, lon_dev, channels), kind),
            pltpu.VMEM(weights.shape, kind),
            pltpu.VMEM((2, chunks, 2) + ana.shape[3:], kind),
            chunk, chunk, chunk, owned, owned, turned, turned,
            dma((7,)), back, dma((PIECES,)), dma((PIECES,)),
            pair, pair,
            dma((chunks, PIECES, lat_n - 1)), dma((chunks, PIECES, lat_n - 1)),
            dma((chunks, BACK, lat_n - 1)), dma((chunks, BACK, lat_n - 1)),
            back, back, back, back, back, back,
        ],
        compiler_params=pltpu.CompilerParams(
            collective_id=0, has_side_effects=True, vmem_limit_bytes=56 * 2**20
        ),
        cost_estimate=pl.CostEstimate(
            flops=12 * 10**9, bytes_accessed=60 * 2**20, transcendentals=0
        ),
    )(grid_field, weights, ana, syn)
    rank = lax.axis_index("lon").astype(jnp.int32).reshape(1)
    return pl.pallas_call(
        synthesis_kernel,
        grid_spec=pltpu.PrefetchScalarGridSpec(
            num_scalar_prefetch=1,
            grid=(lats // LAST,),
            in_specs=[
                pl.BlockSpec((1, 1, out_dev, M), lambda l, r: (r[0], 1, 0, 0)),
                pl.BlockSpec((LAST, M, channels), lambda l, r: (l, 1, 0)),
                pl.BlockSpec(
                    (LAST, out_dev, channels), lambda l, r: (l, 0, 0)
                ),
            ],
            out_specs=pl.BlockSpec((LAST, out_dev, channels), lambda l, r: (l, 0, 0)),
        ),
        out_shape=jax.ShapeDtypeStruct((lats, out_dev, channels), kind),
        compiler_params=pltpu.CompilerParams(vmem_limit_bytes=60 * 2**20),
    )(rank, syn, full, early)


def solution(mesh):
    placed = (P(("grp", "lat"), "lon", None), P(("lon", "lat"), None, None, None))
    lon_count, lat_count = mesh.shape["lon"], mesh.shape["lat"]
    owned_rows = 2 * M // (lon_count * lat_count)
    body = on_device
    if lon_count == 4 and lat_count == 4 and owned_rows % ROWS == 0:
        ana, syn = host_tables(lon_count, lat_count, owned_rows // ROWS)

        def body(grid_field, weights):
            return fast_device(grid_field, weights, jnp.asarray(ana), jnp.asarray(syn))

    return jax.shard_map(
        body,
        mesh=mesh,
        in_specs=placed,
        out_specs=P(("grp", "lat"), "lon", None),
        check_vma=False,
    )
```
